512 devices in a mesh: ctx: 64 (over x, z), head: 8 (over y, core).
Axes of the slice: x: 4, y: 4, z: 16, core: 2. Of those that a mesh axis runs over, the one named last changes fastest.
Arguments:
- queries: bfloat16 [32768, 4096], P('ctx', 'head'), may hold values from -6 to 6
- keys: bfloat16 [32768, 4096], P('ctx', 'head'), may hold values from -6 to 6
- values: bfloat16 [32768, 4096], P('ctx', 'head'), may hold values from -6 to 6
- out_weight: bfloat16 [4096, 4096], P('head', 'ctx'), may hold values from -0.25 to 0.25
Outputs:
- mixed: bfloat16 [32768, 4096], P('ctx', 'head')
The draws below stay inside these ranges and needn't reach their ends.
All inputs are finite; a program needn't handle non-finite values.
Results may differ from the reference program's by a relative error of at most 0.024.
Values may be sent and summed in bfloat16 or wider, within the bound.
No kernel may reach another device: no remote copies, remote signals or barrier semaphores. Data moves between devices by JAX's collectives and lax.ppermute only.
A program may use at most 64 MiB of HBM per device.

```python
import jax
import jax.numpy as jnp
from jax import lax

HEADS = 32
HEAD_DIM = 128
D = 4096
TOK_DEV = 512
TOKENS = 32768
N_CTX = 64
N_HEAD = 8


def raised(entries, stream_key, source, target, parts, factor):
    owner, partner = [(jnp.arange(entries.shape[axis_at]) // (entries.shape[axis_at] // parts)).reshape([-1 if axis == axis_at else 1 for axis in range(entries.ndim)]) for axis_at in (source, target)]
    chosen = jax.random.permutation(stream_key, parts)[partner]
    strong = (owner == chosen) | (owner == (partner + parts // 2) % parts)
    return jnp.where(strong, factor * entries, entries)


def shard_levels(key, extent, cuts, least, high):
    def one(dim, blocks):
        heights = jax.random.uniform(jax.random.fold_in(jax.random.fold_in(key, 6), dim), (blocks,), jnp.float32, least / len(cuts), high / len(cuts))
        return jnp.repeat(jnp.exp(heights), extent[dim] // blocks).reshape((-1,) + (1,) * (len(extent) - dim - 1))

    loudness = one(*cuts[0])
    for cut in cuts[1:]:
        loudness = loudness * one(*cut)
    return loudness


def noise(rng, shape, spread, limit, split=(), kind=jnp.bfloat16):
    drawn = spread * jax.random.normal(rng, shape, jnp.float32)
    if split:
        drawn = drawn * shard_levels(rng, shape, split, -0.22, 0.18)
    return jnp.clip(drawn, -limit, limit).astype(kind)


def bell_draw_with(stream_key, extent, spread, most, split, heavy, held_as=jnp.bfloat16):
    values = spread * jax.random.normal(stream_key, extent, jnp.float32)
    if split:
        values = values * shard_levels(stream_key, extent, split, -0.22, 0.18)
    return jnp.clip(raised(values, jax.random.fold_in(stream_key, 3), *heavy), -most, most).astype(held_as)


def setup_inputs(seed: int = 0) -> dict:
    key_list = jax.random.split(jax.random.key(seed), 5)
    return {
        "queries": noise(key_list[0], (TOKENS, D), 1.0, 6.0, ((0, 64), (1, 8))),
        "keys": noise(key_list[1], (TOKENS, D), 1.0, 6.0, ((0, 64), (1, 8))),
        "values": noise(key_list[2], (TOKENS, D), 1.0, 6.0, ((0, 64), (1, 8))),
        "out_weight": bell_draw_with(key_list[3], (D, D), D ** -0.5, 0.25, ((0, 8), (1, 64)), (0, 1, 64, 4.0)),
    }


def one_head(pieces):
    qh, kh, vh = pieces
    qc = qh.reshape(N_CTX, TOK_DEV, HEAD_DIM).astype(jnp.float32)
    kc = kh.reshape(N_CTX, TOK_DEV, HEAD_DIM).astype(jnp.float32)
    vc = vh.reshape(N_CTX, TOK_DEV, HEAD_DIM).astype(jnp.float32)
    hi = lax.Precision.HIGHEST
    states = jnp.einsum('ctd,cte->cde', kc, vc, precision=hi)
    running = jnp.cumsum(states, axis=0)
    prefix = jnp.concatenate([jnp.zeros((1, HEAD_DIM, HEAD_DIM), jnp.float32), running[:-1]], axis=0)
    prefix_low = prefix.astype(jnp.bfloat16).astype(jnp.float32)
    inter = jnp.einsum('ctd,cde->cte', qc, prefix_low, precision=hi)
    scores = jnp.einsum('ctd,csd->cts', qc, kc, precision=hi)
    causal = jnp.arange(TOK_DEV)[:, None] >= jnp.arange(TOK_DEV)[None, :]
    scores = jnp.where(causal[None], scores, jnp.float32(0.0))
    scores = scores.astype(jnp.bfloat16).astype(jnp.float32)
    intra = jnp.einsum('cts,cse->cte', scores, vc, precision=hi)
    attn = inter + intra
    scale = lax.rsqrt(lax.optimization_barrier(jnp.mean(attn * attn, axis=-1, keepdims=True)) + 1e-06)
    return (attn * scale).astype(jnp.bfloat16).reshape(TOKENS, HEAD_DIM)

def split_heads(array):
    return jnp.transpose(array.reshape(TOKENS, HEADS, HEAD_DIM), (1, 0, 2))

def reference(queries, keys, values, out_weight):
    outs = lax.map(one_head, (split_heads(queries), split_heads(keys), split_heads(values)))
    hidden = jnp.transpose(outs, (1, 0, 2)).reshape(TOKENS, D)
    width = D // N_HEAD
    total = jnp.zeros((TOKENS, D), jnp.float32)
    for group in range(N_HEAD):
        part = jnp.dot(hidden[:, group * width:(group + 1) * width], out_weight[group * width:(group + 1) * width], preferred_element_type=jnp.float32)
        total = total + lax.optimization_barrier(part.astype(jnp.bfloat16)).astype(jnp.float32)
    return total.astype(jnp.bfloat16)
```

```python
import jax
import jax.numpy as jnp
from jax import lax
from jax.experimental import pallas as pl
from jax.experimental.pallas import tpu as pltpu
from jax.sharding import Mesh, PartitionSpec as P

HEAD_DIM = 128
NX, NZ, NY, NC = 4, 16, 4, 2
N_CTX = NX * NZ
BF = jnp.bfloat16
F32 = jnp.float32
VMEM = 48 * 1024 * 1024


def params():
    return pltpu.CompilerParams(vmem_limit_bytes=VMEM)


def whole(n):
    return [pl.BlockSpec(memory_space=pltpu.VMEM)] * n


def states_kernel(k_ref, v_ref, o_ref):
    for h in range(k_ref.shape[1] // HEAD_DIM):
        cols = slice(h * HEAD_DIM, (h + 1) * HEAD_DIM)
        o_ref[cols, :] = lax.dot_general(
            k_ref[:, cols], v_ref[:, cols], (((0,), (0,)), ((), ())), preferred_element_type=F32
        ).astype(BF)


def scan_kernel(s_ref, o_ref):
    total = jnp.zeros(s_ref.shape[1:], F32)
    for c in range(s_ref.shape[0]):
        o_ref[c] = total.astype(BF)
        total = total + s_ref[c].astype(F32)


def attention_kernel(q_ref, k_ref, v_ref, p_ref, o_ref):
    rows = q_ref.shape[0]
    blk = 256
    t = lax.broadcasted_iota(jnp.int32, (blk, blk), 0)
    s = lax.broadcasted_iota(jnp.int32, (blk, blk), 1)
    causal = t >= s
    for h in range(q_ref.shape[1] // HEAD_DIM):
        cols = slice(h * HEAD_DIM, (h + 1) * HEAD_DIM)
        prefix = p_ref[cols, :]
        for i in range(rows // blk):
            here = slice(i * blk, (i + 1) * blk)
            q = q_ref[here, cols]
            attn = jnp.dot(q, prefix, preferred_element_type=F32)
            for j in range(i + 1):
                there = slice(j * blk, (j + 1) * blk)
                scores = lax.dot_general(
                    q, k_ref[there, cols], (((1,), (1,)), ((), ())), preferred_element_type=F32
                )
                if i == j:
                    scores = jnp.where(causal, scores, 0.0)
                attn += jnp.dot(scores.astype(BF), v_ref[there, cols], preferred_element_type=F32)
            scale = lax.rsqrt(jnp.mean(attn * attn, axis=-1, keepdims=True) + 1e-06)
            o_ref[here, cols] = (attn * scale).astype(BF)


def projection_kernel(order_ref, *refs):
    hidden, (w_ref, o_ref) = refs[:8], refs[8:]
    zl = NZ // NC
    total = None
    for n, h_ref in enumerate(hidden):
        core, slot = order_ref[2 * n], order_ref[2 * n + 1]
        w = w_ref[pl.ds(core * zl, zl), slot].reshape(zl * w_ref.shape[2], w_ref.shape[3])
        part = lax.dot_general(h_ref[...], w, (((1,), (1,)), ((), ())), preferred_element_type=F32)
        total = part if total is None else total + part
    o_ref[...] = total.astype(BF)


def linear(x, z, y, c):
    return ((x * NZ + z) * NY + y) * NC + c


AXES = ("x", "z", "y", "c")


def weight_pairs(k):
    zl = NZ // NC
    pairs = []
    for x in range(NX):
        for z in range(NZ):
            for y in range(NY):
                for c in range(NC):
                    pairs.append(
                        (linear(x, z, y, c), linear((y + k) % NX, c * zl + z % zl, x, z // zl))
                    )
    return pairs


def local(queries, keys, values, out_weight):
    rows, width = queries.shape
    w = out_weight.T
    w4 = jnp.stack([lax.ppermute(w, AXES, weight_pairs(k)) for k in range(NX)])
    states = pl.pallas_call(
        states_kernel,
        out_shape=jax.ShapeDtypeStruct((width, HEAD_DIM), BF),
        in_specs=whole(2), out_specs=whole(1)[0], compiler_params=params(),
    )(keys, values)
    states, w4 = lax.optimization_barrier((states, w4))
    w_all = lax.all_gather(w4, "z")
    part = width // N_CTX
    mine = lax.all_to_all(states.reshape(N_CTX, part, HEAD_DIM), ("x", "z"), 0, 0)
    scanned = pl.pallas_call(
        scan_kernel,
        out_shape=jax.ShapeDtypeStruct(mine.shape, BF),
        in_specs=whole(1), out_specs=whole(1)[0], compiler_params=params(),
    )(mine)
    prefix = lax.all_to_all(scanned, ("x", "z"), 0, 0).reshape(width, HEAD_DIM)
    hidden = pl.pallas_call(
        attention_kernel,
        out_shape=jax.ShapeDtypeStruct((rows, width), BF),
        in_specs=whole(4), out_specs=whole(1)[0], compiler_params=params(),
    )(queries, keys, values, prefix)

    def along(axis, n, d, a):
        return lax.ppermute(a, axis, [(i, (i + d) % n) for i in range(n)])

    blocks = [hidden] + [along("y", NY, d, hidden) for d in (1, 3, 2)]
    others = [along("c", NC, 1, b) for b in blocks]
    me_x, me_y, me_c = lax.axis_index("x"), lax.axis_index("y"), lax.axis_index("c")
    order = []
    for flip in (0, 1):
        for d in (0, 1, 3, 2):
            source_y = (me_y - d) % NY
            order += [(me_c + flip) % NC, (me_x - source_y) % NX]
    order = jnp.stack(order).astype(jnp.int32)
    return pl.pallas_call(
        projection_kernel,
        out_shape=jax.ShapeDtypeStruct((rows, width), BF),
        in_specs=[pl.BlockSpec(memory_space=pltpu.SMEM)] + whole(9),
        out_specs=whole(1)[0], compiler_params=params(),
    )(order, *blocks, *others, w_all)


def solution(mesh):
    fine = Mesh(mesh.devices.reshape(NX, NZ, NY, NC), AXES)
    ctx, head = ("x", "z"), ("y", "c")
    in_specs = (P(ctx, head), P(ctx, head), P(ctx, head), P(head, ctx))
    return jax.shard_map(local, mesh=fine, in_specs=in_specs, out_specs=P(ctx, head), check_vma=False)
```

```python
import jax
import jax.numpy as jnp
from jax import lax
from jax.experimental import pallas as pl
from jax.experimental.pallas import tpu as pltpu
from jax.sharding import Mesh, PartitionSpec as P

HEAD_DIM = 128
NX, NZ, NY, NC = 4, 16, 4, 2
N_CTX = NX * NZ
BF = jnp.bfloat16
F32 = jnp.float32


def params():
    return pltpu.CompilerParams(vmem_limit_bytes=48 * 1024 * 1024)


def states_kernel(k_ref, v_ref, o_ref):
    o_ref[...] = lax.dot_general(
        k_ref[...], v_ref[...], (((0,), (0,)), ((), ())), preferred_element_type=F32
    ).astype(BF)


def scan_kernel(s_ref, o_ref):
    total = jnp.zeros(s_ref.shape[1:], F32)
    for c in range(s_ref.shape[0]):
        o_ref[c] = total.astype(BF)
        total = total + s_ref[c].astype(F32)


def attention_kernel(q_ref, k_ref, v_ref, p_ref, o_ref):
    rows = q_ref.shape[0]
    blk = 256
    t = lax.broadcasted_iota(jnp.int32, (blk, blk), 0)
    s = lax.broadcasted_iota(jnp.int32, (blk, blk), 1)
    causal = t >= s
    prefix = p_ref[...]
    for i in range(rows // blk):
        here = slice(i * blk, (i + 1) * blk)
        q = q_ref[here, :]
        attn = jnp.dot(q, prefix, preferred_element_type=F32)
        for j in range(i + 1):
            there = slice(j * blk, (j + 1) * blk)
            scores = lax.dot_general(
                q, k_ref[there, :], (((1,), (1,)), ((), ())), preferred_element_type=F32
            )
            if i == j:
                scores = jnp.where(causal, scores, 0.0)
            attn += jnp.dot(scores.astype(BF), v_ref[there, :], preferred_element_type=F32)
        scale = lax.rsqrt(jnp.mean(attn * attn, axis=-1, keepdims=True) + 1e-06)
        hidden = (attn * scale).astype(BF)
        for n in range(o_ref.shape[0]):
            o_ref[n, here, :] = hidden


def projection_kernel(order_ref, h_ref, w_ref, o_ref):
    blocks, _, cols, depth = w_ref.shape
    total = None
    for y in range(h_ref.shape[0]):
        w = w_ref[:, order_ref[1 + y]].reshape(blocks * cols, depth)
        part = lax.dot_general(h_ref[y], w, (((1,), (1,)), ((), ())), preferred_element_type=F32)
        total = part if total is None else total + part
    o_ref[...] = total.astype(o_ref.dtype)


def add_kernel(a_ref, b_ref, o_ref):
    o_ref[...] = (a_ref[...] + b_ref[...].astype(F32)).astype(BF)


def project(order, hidden, w_all, dtype):
    sources, rows, depth = hidden.shape
    slots, cols = w_all.shape[1:3]
    zb = 4
    width = NZ // NC * cols
    steps = NZ // NC // zb
    return pl.pallas_call(
        projection_kernel,
        grid_spec=pltpu.PrefetchScalarGridSpec(
            num_scalar_prefetch=1,
            grid=(steps,),
            in_specs=[
                pl.BlockSpec((sources, rows, depth), lambda n, order: (0, 0, 0)),
                pl.BlockSpec((zb, slots, cols, depth), lambda n, order: (order[0] * steps + n, 0, 0, 0)),
            ],
            out_specs=pl.BlockSpec((rows, zb * cols), lambda n, order: (0, n)),
        ),
        out_shape=jax.ShapeDtypeStruct((rows, width), dtype),
        compiler_params=params(),
    )(order, hidden, w_all)


AXES = ("x", "z", "y", "c")


def local(queries, keys, values, out_weight):
    rows, width = queries.shape
    heads = width // HEAD_DIM
    me_x, me_c = lax.axis_index("x"), lax.axis_index("c")

    w = out_weight.T
    w4 = jnp.stack([
        lax.ppermute(
            w, ("x", "y"),
            [(x * NY + y, (y + k) % NX * NY + x) for x in range(NX) for y in range(NY)],
        )
        for k in range(NX)
    ])
    by_head = pl.BlockSpec((rows, HEAD_DIM), lambda h: (0, h))
    state = pl.BlockSpec((HEAD_DIM, HEAD_DIM), lambda h: (h, 0))
    states = pl.pallas_call(
        states_kernel,
        grid=(heads,),
        out_shape=jax.ShapeDtypeStruct((width, HEAD_DIM), BF),
        in_specs=[by_head, by_head], out_specs=state, compiler_params=params(),
    )(keys, values)
    states, w4 = lax.optimization_barrier((states, w4))
    w_all = lax.all_gather(w4, "z")
    part = width // N_CTX
    mine = lax.all_to_all(states.reshape(N_CTX, part, HEAD_DIM), ("x", "z"), 0, 0)
    scanned = pl.pallas_call(
        scan_kernel, out_shape=jax.ShapeDtypeStruct(mine.shape, BF), compiler_params=params(),
    )(mine)
    prefix = lax.all_to_all(scanned, ("x", "z"), 0, 0).reshape(width, HEAD_DIM)
    hidden = pl.pallas_call(
        attention_kernel,
        grid=(heads,),
        out_shape=jax.ShapeDtypeStruct((NY, rows, width), BF),
        in_specs=[by_head, by_head, by_head, state],
        out_specs=pl.BlockSpec((NY, rows, HEAD_DIM), lambda h: (0, 0, h)),
        compiler_params=params(),
    )(queries, keys, values, prefix)
    hidden = lax.all_to_all(hidden, "y", 0, 0)
    slots = [(me_x - y) % NX for y in range(NY)]
    away = jnp.stack([1 - me_c] + slots).astype(jnp.int32)
    home = jnp.stack([me_c] + slots).astype(jnp.int32)
    other = project(away, hidden, w_all, BF)
    other = lax.ppermute(other, "c", [(0, 1), (1, 0)])
    own = project(home, hidden, w_all, F32)
    tile = pl.BlockSpec((rows // 2, width), lambda n: (n, 0))
    return pl.pallas_call(
        add_kernel,
        grid=(2,),
        out_shape=jax.ShapeDtypeStruct((rows, width), BF),
        in_specs=[tile, tile], out_specs=tile, compiler_params=params(),
    )(own, other)


def solution(mesh):
    fine = Mesh(mesh.devices.reshape(NX, NZ, NY, NC), AXES)
    ctx, head = ("x", "z"), ("y", "c")
    in_specs = (P(ctx, head), P(ctx, head), P(ctx, head), P(head, ctx))
    return jax.shard_map(local, mesh=fine, in_specs=in_specs, out_specs=P(ctx, head), check_vma=False)
```

```python
import jax
import jax.numpy as jnp
from jax import lax
from jax.experimental import pallas as pl
from jax.experimental.pallas import tpu as pltpu
from jax.sharding import Mesh, PartitionSpec as P

HEAD_DIM = 128
NX, NZ, NY, NC = 4, 16, 4, 2
N_CTX = NX * NZ
BF = jnp.bfloat16
F32 = jnp.float32


def params():
    return pltpu.CompilerParams(vmem_limit_bytes=48 * 1024 * 1024)


def states_kernel(k_ref, v_ref, o_ref):
    o_ref[...] = lax.dot_general(
        k_ref[...], v_ref[...], (((0,), (0,)), ((), ())), preferred_element_type=F32
    ).astype(BF)


def scan_kernel(s_ref, o_ref):
    total = jnp.zeros(s_ref.shape[1:], F32)
    for c in range(s_ref.shape[0]):
        o_ref[c] = total.astype(BF)
        total = total + s_ref[c].astype(F32)


def attention_kernel(q_ref, k_ref, v_ref, p_ref, o_ref):
    rows = q_ref.shape[0]
    blk = 256
    t = lax.broadcasted_iota(jnp.int32, (blk, blk), 0)
    s = lax.broadcasted_iota(jnp.int32, (blk, blk), 1)
    causal = t >= s
    prefix = p_ref[...]
    for i in range(rows // blk):
        here = slice(i * blk, (i + 1) * blk)
        q = q_ref[here, :]
        attn = jnp.dot(q, prefix, preferred_element_type=F32)
        for j in range(i + 1):
            there = slice(j * blk, (j + 1) * blk)
            scores = lax.dot_general(
                q, k_ref[there, :], (((1,), (1,)), ((), ())), preferred_element_type=F32
            )
            if i == j:
                scores = jnp.where(causal, scores, 0.0)
            attn += jnp.dot(scores.astype(BF), v_ref[there, :], preferred_element_type=F32)
        scale = lax.rsqrt(jnp.mean(attn * attn, axis=-1, keepdims=True) + 1e-06)
        hidden = (attn * scale).astype(BF)
        for n in range(o_ref.shape[0]):
            o_ref[n, here, :] = hidden


def projection_kernel(order_ref, h_ref, w_ref, o_ref):
    blocks, sources, cols, depth = w_ref.shape
    total = None
    for y in range(sources):
        w = w_ref[:, y].reshape(blocks * cols, depth)
        part = lax.dot_general(h_ref[y], w, (((1,), (1,)), ((), ())), preferred_element_type=F32)
        total = part if total is None else total + part
    o_ref[...] = total.astype(o_ref.dtype)


def add_kernel(a_ref, b_ref, o_ref):
    o_ref[...] = (a_ref[...] + b_ref[...].astype(F32)).astype(BF)


def project(order, hidden, w_all, dtype):
    sources, rows, depth = hidden.shape
    cols = w_all.shape[2]
    zb = 4
    width = NZ // NC * cols
    steps = NZ // NC // zb
    return pl.pallas_call(
        projection_kernel,
        grid_spec=pltpu.PrefetchScalarGridSpec(
            num_scalar_prefetch=1,
            grid=(steps,),
            in_specs=[
                pl.BlockSpec(memory_space=pltpu.VMEM),
                pl.BlockSpec((zb, sources, cols, depth), lambda n, order: (order[0] * steps + n, 0, 0, 0)),
            ],
            out_specs=pl.BlockSpec((rows, zb * cols), lambda n, order: (0, n)),
        ),
        out_shape=jax.ShapeDtypeStruct((rows, width), dtype),
        cost_estimate=pl.CostEstimate(
            flops=2 * rows * width * sources * depth, bytes_accessed=4 << 20, transcendentals=0
        ),
        compiler_params=params(),
    )(order, hidden, w_all)


AXES = ("x", "z", "y", "c")


def local(queries, keys, values, out_weight):
    rows, width = queries.shape
    heads = width // HEAD_DIM
    me_c = lax.axis_index("c")

    w = lax.ppermute(
        out_weight.T, ("x", "y"),
        [(x * NY + y, y * NY + x) for x in range(NX) for y in range(NY)],
    )
    by_head = pl.BlockSpec((rows, HEAD_DIM), lambda h: (0, h))
    state = pl.BlockSpec((HEAD_DIM, HEAD_DIM), lambda h: (h, 0))
    states = pl.pallas_call(
        states_kernel,
        grid=(heads,),
        out_shape=jax.ShapeDtypeStruct((width, HEAD_DIM), BF),
        in_specs=[by_head, by_head], out_specs=state, compiler_params=params(),
    )(keys, values)
    states, w = lax.optimization_barrier((states, w))
    w4 = lax.all_to_all(jnp.broadcast_to(w[None], (NX,) + w.shape), "x", 0, 0)
    states, w4 = lax.optimization_barrier((states, w4))
    w_all = lax.all_gather(w4, "z")
    part = width // N_CTX
    mine = lax.all_to_all(states.reshape(N_CTX, part, HEAD_DIM), ("x", "z"), 0, 0)
    scanned = pl.pallas_call(
        scan_kernel, out_shape=jax.ShapeDtypeStruct(mine.shape, BF), compiler_params=params(),
    )(mine)
    prefix = lax.all_to_all(scanned, ("x", "z"), 0, 0).reshape(width, HEAD_DIM)
    hidden = pl.pallas_call(
        attention_kernel,
        grid=(heads,),
        out_shape=jax.ShapeDtypeStruct((NY, rows, width), BF),
        in_specs=[by_head, by_head, by_head, state],
        out_specs=pl.BlockSpec((NY, rows, HEAD_DIM), lambda h: (0, 0, h)),
        compiler_params=params(),
    )(queries, keys, values, prefix)
    hidden = lax.all_to_all(hidden, "y", 0, 0)
    away = (1 - me_c).astype(jnp.int32).reshape(1)
    home = me_c.astype(jnp.int32).reshape(1)
    other = project(away, hidden, w_all, BF)
    other = lax.ppermute(other, "c", [(0, 1), (1, 0)])
    own = project(home, hidden, w_all, F32)
    tile = pl.BlockSpec((rows // 2, width), lambda n: (n, 0))
    return pl.pallas_call(
        add_kernel,
        grid=(2,),
        out_shape=jax.ShapeDtypeStruct((rows, width), BF),
        in_specs=[tile, tile], out_specs=tile, compiler_params=params(),
    )(own, other)


def solution(mesh):
    fine = Mesh(mesh.devices.reshape(NX, NZ, NY, NC), AXES)
    ctx, head = ("x", "z"), ("y", "c")
    in_specs = (P(ctx, head), P(ctx, head), P(ctx, head), P(head, ctx))
    return jax.shard_map(local, mesh=fine, in_specs=in_specs, out_specs=P(ctx, head), check_vma=False)
```

```python
import jax
import jax.numpy as jnp
from jax import lax
from jax.experimental import pallas as pl
from jax.experimental.pallas import tpu as pltpu
from jax.sharding import Mesh, PartitionSpec as P

HEAD_DIM = 128
NX, NZ, NY, NC = 4, 16, 4, 2
N_CTX = NX * NZ
BF = jnp.bfloat16
F32 = jnp.float32


def params():
    return pltpu.CompilerParams(vmem_limit_bytes=48 * 1024 * 1024)


def states_kernel(k_ref, v_ref, o_ref):
    o_ref[...] = lax.dot_general(
        k_ref[...], v_ref[...], (((0,), (0,)), ((), ())), preferred_element_type=F32
    ).astype(BF)


def scan_kernel(s_ref, o_ref):
    total = jnp.zeros(s_ref.shape[1:], F32)
    for c in range(s_ref.shape[0]):
        o_ref[c] = total.astype(BF)
        total = total + s_ref[c].astype(F32)


def attention_kernel(q_ref, k_ref, v_ref, p_ref, o_ref):
    rows = q_ref.shape[0]
    blk = 256
    t = lax.broadcasted_iota(jnp.int32, (blk, blk), 0)
    s = lax.broadcasted_iota(jnp.int32, (blk, blk), 1)
    causal = t >= s
    prefix = p_ref[...]
    for i in range(rows // blk):
        here = slice(i * blk, (i + 1) * blk)
        q = q_ref[here, :]
        attn = jnp.dot(q, prefix, preferred_element_type=F32)
        for j in range(i + 1):
            there = slice(j * blk, (j + 1) * blk)
            scores = lax.dot_general(
                q, k_ref[there, :], (((1,), (1,)), ((), ())), preferred_element_type=F32
            )
            if i == j:
                scores = jnp.where(causal, scores, 0.0)
            attn += jnp.dot(scores.astype(BF), v_ref[there, :], preferred_element_type=F32)
        scale = lax.rsqrt(jnp.mean(attn * attn, axis=-1, keepdims=True) + 1e-06)
        hidden = (attn * scale).astype(BF)
        for n in range(o_ref.shape[0]):
            o_ref[n, here, :] = hidden


def projection_kernel(core_ref, own_ref, other_ref, w_ref, o_ref, acc_ref):
    blocks, _, sources, cols, depth = w_ref.shape

    def part(h_ref):
        total = None
        for y in range(sources):
            w = w_ref[:, 0, y].reshape(blocks * cols, depth)
            one = lax.dot_general(h_ref[y], w, (((1,), (1,)), ((), ())), preferred_element_type=F32)
            total = one if total is None else total + one
        return total

    @pl.when(pl.program_id(1) == 0)
    def _():
        acc_ref[...] = part(own_ref)

    @pl.when(pl.program_id(1) == 1)
    def _():
        o_ref[...] = (acc_ref[...] + part(other_ref)).astype(o_ref.dtype)


def project(core, own, other, w_all):
    sources, rows, depth = own.shape
    cols = w_all.shape[3]
    zb = 4
    steps = NZ // NC // zb
    return pl.pallas_call(
        projection_kernel,
        grid_spec=pltpu.PrefetchScalarGridSpec(
            num_scalar_prefetch=1,
            grid=(steps, NC),
            in_specs=[pl.BlockSpec(memory_space=pltpu.VMEM)] * 2 + [
                pl.BlockSpec(
                    (zb, 1, sources, cols, depth),
                    lambda n, k, core: (core[0] * steps + n, core[0] ^ k, 0, 0, 0),
                ),
            ],
            out_specs=pl.BlockSpec((rows, zb * cols), lambda n, k, core: (0, n)),
            scratch_shapes=[pltpu.VMEM((rows, zb * cols), F32)],
        ),
        out_shape=jax.ShapeDtypeStruct((rows, NZ // NC * cols), BF),
        compiler_params=params(),
    )(core, own, other, w_all)


AXES = ("x", "z", "y", "c")


def local(queries, keys, values, out_weight):
    rows, width = queries.shape
    heads = width // HEAD_DIM
    me_c = lax.axis_index("c")

    w = lax.ppermute(
        out_weight.T, ("x", "y"),
        [(x * NY + y, y * NY + x) for x in range(NX) for y in range(NY)],
    )
    by_head = pl.BlockSpec((rows, HEAD_DIM), lambda h: (0, h))
    state = pl.BlockSpec((HEAD_DIM, HEAD_DIM), lambda h: (h, 0))
    states = pl.pallas_call(
        states_kernel,
        grid=(heads,),
        out_shape=jax.ShapeDtypeStruct((width, HEAD_DIM), BF),
        in_specs=[by_head, by_head], out_specs=state, compiler_params=params(),
    )(keys, values)
    states, w = lax.optimization_barrier((states, w))
    w4 = lax.all_to_all(jnp.broadcast_to(w[None], (NX,) + w.shape), "x", 0, 0)
    states, w4 = lax.optimization_barrier((states, w4))
    w_all = lax.all_gather(w4, ("z", "c")).reshape((NZ, NC) + w4.shape)
    part = width // N_CTX
    mine = lax.all_to_all(states.reshape(N_CTX, part, HEAD_DIM), ("x", "z"), 0, 0)
    scanned = pl.pallas_call(
        scan_kernel, out_shape=jax.ShapeDtypeStruct(mine.shape, BF), compiler_params=params(),
    )(mine)
    prefix = lax.all_to_all(scanned, ("x", "z"), 0, 0).reshape(width, HEAD_DIM)
    hidden = pl.pallas_call(
        attention_kernel,
        grid=(heads,),
        out_shape=jax.ShapeDtypeStruct((NY, rows, width), BF),
        in_specs=[by_head, by_head, by_head, state],
        out_specs=pl.BlockSpec((NY, rows, HEAD_DIM), lambda h: (0, 0, h)),
        compiler_params=params(),
    )(queries, keys, values, prefix)
    hidden = lax.all_to_all(hidden, "y", 0, 0)
    other = lax.ppermute(hidden, "c", [(0, 1), (1, 0)])
    return project(me_c.astype(jnp.int32).reshape(1), hidden, other, w_all)


def solution(mesh):
    fine = Mesh(mesh.devices.reshape(NX, NZ, NY, NC), AXES)
    ctx, head = ("x", "z"), ("y", "c")
    in_specs = (P(ctx, head), P(ctx, head), P(ctx, head), P(head, ctx))
    return jax.shard_map(local, mesh=fine, in_specs=in_specs, out_specs=P(ctx, head), check_vma=False)
```

```python
import jax
import jax.numpy as jnp
from jax import lax
from jax.experimental import pallas as pl
from jax.experimental.pallas import tpu as pltpu
from jax.sharding import Mesh, PartitionSpec as P

HEAD_DIM = 128
NX, NZ, NY, NC = 4, 16, 4, 2
N_CTX = NX * NZ
HOME = 2
BF = jnp.bfloat16
F32 = jnp.float32


def params():
    return pltpu.CompilerParams(vmem_limit_bytes=48 * 1024 * 1024)


def states_kernel(k_ref, v_ref, o_ref):
    o_ref[...] = lax.dot_general(
        k_ref[...], v_ref[...], (((0,), (0,)), ((), ())), preferred_element_type=F32
    ).astype(BF)


def scan_kernel(s_ref, o_ref):
    total = jnp.zeros(s_ref.shape[1:], F32)
    for c in range(s_ref.shape[0]):
        o_ref[c] = total.astype(BF)
        total = total + s_ref[c].astype(F32)


def attention_kernel(q_ref, k_ref, v_ref, p_ref, o_ref):
    rows = q_ref.shape[0]
    blk = 256
    t = lax.broadcasted_iota(jnp.int32, (blk, blk), 0)
    s = lax.broadcasted_iota(jnp.int32, (blk, blk), 1)
    causal = t >= s
    prefix = p_ref[...]
    for i in range(rows // blk):
        here = slice(i * blk, (i + 1) * blk)
        q = q_ref[here, :]
        attn = jnp.dot(q, prefix, preferred_element_type=F32)
        for j in range(i + 1):
            there = slice(j * blk, (j + 1) * blk)
            scores = lax.dot_general(
                q, k_ref[there, :], (((1,), (1,)), ((), ())), preferred_element_type=F32
            )
            if i == j:
                scores = jnp.where(causal, scores, 0.0)
            attn += jnp.dot(scores.astype(BF), v_ref[there, :], preferred_element_type=F32)
        scale = lax.rsqrt(jnp.mean(attn * attn, axis=-1, keepdims=True) + 1e-06)
        hidden = (attn * scale).astype(BF)
        for n in range(o_ref.shape[0]):
            o_ref[n, here, :] = hidden


def projection_kernel(core_ref, own_ref, other_ref, w_ref, o_ref, acc_ref):
    blocks, _, sources, cols, depth = w_ref.shape

    def part(h_ref):
        total = None
        for y in range(sources):
            w = w_ref[:, 0, (y + HOME) % NX].reshape(blocks * cols, depth)
            one = lax.dot_general(h_ref[y], w, (((1,), (1,)), ((), ())), preferred_element_type=F32)
            total = one if total is None else total + one
        return total

    @pl.when(pl.program_id(1) == 0)
    def _():
        acc_ref[...] = part(own_ref)

    @pl.when(pl.program_id(1) == 1)
    def _():
        o_ref[...] = (acc_ref[...] + part(other_ref)).astype(o_ref.dtype)


def project(core, own, other, w_all):
    sources, rows, depth = own.shape
    cols = w_all.shape[3]
    zb = 8
    steps = NZ // NC // zb
    return pl.pallas_call(
        projection_kernel,
        grid_spec=pltpu.PrefetchScalarGridSpec(
            num_scalar_prefetch=1,
            grid=(steps, NC),
            in_specs=[pl.BlockSpec(memory_space=pltpu.VMEM)] * 2 + [
                pl.BlockSpec(
                    (zb, 1, sources, cols, depth),
                    lambda n, k, core: (core[0] * steps + n, core[0] ^ k, 0, 0, 0),
                ),
            ],
            out_specs=pl.BlockSpec((rows, zb * cols), lambda n, k, core: (0, n)),
            scratch_shapes=[pltpu.VMEM((rows, zb * cols), F32)],
        ),
        out_shape=jax.ShapeDtypeStruct((rows, NZ // NC * cols), BF),
        compiler_params=params(),
    )(core, own, other, w_all)


AXES = ("x", "z", "y", "c")


def local(queries, keys, values, out_weight):
    rows, width = queries.shape
    heads = width // HEAD_DIM
    me_c = lax.axis_index("c")

    w = lax.ppermute(
        out_weight.T, ("x", "y"),
        [(x * NY + y, (y + HOME) % NX * NY + x) for x in range(NX) for y in range(NY)],
    )
    by_head = pl.BlockSpec((rows, HEAD_DIM), lambda h: (0, h))
    state = pl.BlockSpec((HEAD_DIM, HEAD_DIM), lambda h: (h, 0))
    states = pl.pallas_call(
        states_kernel,
        grid=(heads,),
        out_shape=jax.ShapeDtypeStruct((width, HEAD_DIM), BF),
        in_specs=[by_head, by_head], out_specs=state, compiler_params=params(),
    )(keys, values)
    states, w = lax.optimization_barrier((states, w))
    w4 = lax.all_to_all(jnp.broadcast_to(w[None], (NX,) + w.shape), "x", 0, 0)
    states, w4 = lax.optimization_barrier((states, w4))
    w_all = lax.all_gather(w4, ("z", "c")).reshape((NZ, NC) + w4.shape)
    part = width // N_CTX
    mine = lax.all_to_all(states.reshape(N_CTX, part, HEAD_DIM), ("x", "z"), 0, 0)
    scanned = pl.pallas_call(
        scan_kernel, out_shape=jax.ShapeDtypeStruct(mine.shape, BF), compiler_params=params(),
    )(mine)
    prefix = lax.all_to_all(scanned, ("x", "z"), 0, 0).reshape(width, HEAD_DIM)
    hidden = pl.pallas_call(
        attention_kernel,
        grid=(heads,),
        out_shape=jax.ShapeDtypeStruct((NY, rows, width), BF),
        in_specs=[by_head, by_head, by_head, state],
        out_specs=pl.BlockSpec((NY, rows, HEAD_DIM), lambda h: (0, 0, h)),
        compiler_params=params(),
    )(queries, keys, values, prefix)
    hidden = lax.all_to_all(hidden, "y", 0, 0)
    other = lax.ppermute(hidden, "c", [(0, 1), (1, 0)])
    return project(me_c.astype(jnp.int32).reshape(1), hidden, other, w_all)


def solution(mesh):
    fine = Mesh(mesh.devices.reshape(NX, NZ, NY, NC), AXES)
    ctx, head = ("x", "z"), ("y", "c")
    in_specs = (P(ctx, head), P(ctx, head), P(ctx, head), P(head, ctx))
    return jax.shard_map(local, mesh=fine, in_specs=in_specs, out_specs=P(ctx, head), check_vma=False)
```

```python
import jax
import jax.numpy as jnp
from jax import lax
from jax.experimental import pallas as pl
from jax.experimental.pallas import tpu as pltpu
from jax.sharding import Mesh, PartitionSpec as P

HEAD_DIM = 128
NX, NZ, NY, NC = 4, 16, 4, 2
N_CTX = NX * NZ
HOME = 2
BF = jnp.bfloat16
F32 = jnp.float32


def params():
    return pltpu.CompilerParams(vmem_limit_bytes=48 * 1024 * 1024)


def states_kernel(k_ref, v_ref, o_ref):
    o_ref[...] = lax.dot_general(
        k_ref[...], v_ref[...], (((0,), (0,)), ((), ())), preferred_element_type=F32
    ).astype(BF)


def scan_kernel(s_ref, o_ref):
    total = jnp.zeros(s_ref.shape[1:], F32)
    for c in range(s_ref.shape[0]):
        o_ref[c] = total.astype(BF)
        total = total + s_ref[c].astype(F32)


def attention_kernel(q_ref, k_ref, v_ref, p_ref, o_ref):
    rows = q_ref.shape[0]
    blk = 256
    t = lax.broadcasted_iota(jnp.int32, (blk, blk), 0)
    s = lax.broadcasted_iota(jnp.int32, (blk, blk), 1)
    causal = t >= s
    prefix = p_ref[...]
    for i in range(rows // blk):
        here = slice(i * blk, (i + 1) * blk)
        q = q_ref[here, :]
        attn = jnp.dot(q, prefix, preferred_element_type=F32)
        for j in range(i + 1):
            there = slice(j * blk, (j + 1) * blk)
            scores = lax.dot_general(
                q, k_ref[there, :], (((1,), (1,)), ((), ())), preferred_element_type=F32
            )
            if i == j:
                scores = jnp.where(causal, scores, 0.0)
            attn += jnp.dot(scores.astype(BF), v_ref[there, :], preferred_element_type=F32)
        scale = lax.rsqrt(jnp.mean(attn * attn, axis=-1, keepdims=True) + 1e-06)
        hidden = (attn * scale).astype(BF)
        for n in range(o_ref.shape[0]):
            o_ref[n, here, :] = hidden


def projection_kernel(core_ref, own_ref, far_ref, w_ref, o_ref, *scratch):
    parts, other_ref, acc_ref, sem = scratch[:4], scratch[4], scratch[5], scratch[6]
    core = core_ref[0]
    blocks, _, per, cols, depth = parts[0].shape
    rows_of = [(k, first) for k in range(NC) for first in range(0, NY, per)]
    copies = [
        pltpu.make_async_copy(
            w_ref.at[pl.ds(core * blocks, blocks), pl.ds(core ^ k, 1), pl.ds(first, per)], part, sem.at[n]
        )
        for n, ((k, first), part) in enumerate(zip(rows_of, parts))
    ]
    other = pltpu.make_async_copy(far_ref, other_ref, sem.at[len(copies)])
    copies[0].start()
    copies[1].start()
    other.start()
    copies[2].start()
    copies[3].start()
    for n, (k, first) in enumerate(rows_of):
        copies[n].wait()
        if n == len(rows_of) // NC:
            other.wait()
        h_ref = own_ref if k == 0 else other_ref
        total = None
        for i in range(per):
            w = parts[n][:, 0, i].reshape(blocks * cols, depth)
            one = lax.dot_general(
                h_ref[(first + i - HOME) % NY], w, (((1,), (1,)), ((), ())), preferred_element_type=F32
            )
            total = one if total is None else total + one
        if n == 0:
            acc_ref[...] = total
        elif n < len(rows_of) - 1:
            acc_ref[...] += total
        else:
            o_ref[...] = (acc_ref[...] + total).astype(o_ref.dtype)


def project(core, own, other, w_all):
    sources, rows, depth = own.shape
    cols = w_all.shape[3]
    blocks, per = NZ // NC, NY // 2
    anywhere, vmem = pl.BlockSpec(memory_space=pl.ANY), pl.BlockSpec(memory_space=pltpu.VMEM)
    return pl.pallas_call(
        projection_kernel,
        in_specs=[pl.BlockSpec(memory_space=pltpu.SMEM), vmem, anywhere, anywhere],
        out_specs=vmem,
        scratch_shapes=[pltpu.VMEM((blocks, 1, per, cols, depth), BF)] * 4 + [
            pltpu.VMEM((sources, rows, depth), BF),
            pltpu.VMEM((rows, blocks * cols), F32),
            pltpu.SemaphoreType.DMA((5,)),
        ],
        out_shape=jax.ShapeDtypeStruct((rows, blocks * cols), BF),
        compiler_params=params(),
    )(core, own, other, w_all)


AXES = ("x", "z", "y", "c")


def local(queries, keys, values, out_weight):
    rows, width = queries.shape
    heads = width // HEAD_DIM
    me_c = lax.axis_index("c")

    w = lax.ppermute(
        out_weight.T, ("x", "y"),
        [(x * NY + y, (y + HOME) % NX * NY + x) for x in range(NX) for y in range(NY)],
    )
    by_head = pl.BlockSpec((rows, HEAD_DIM), lambda h: (0, h))
    state = pl.BlockSpec((HEAD_DIM, HEAD_DIM), lambda h: (h, 0))
    states = pl.pallas_call(
        states_kernel,
        grid=(heads,),
        out_shape=jax.ShapeDtypeStruct((width, HEAD_DIM), BF),
        in_specs=[by_head, by_head], out_specs=state, compiler_params=params(),
    )(keys, values)
    states, w = lax.optimization_barrier((states, w))
    w4 = lax.all_to_all(jnp.broadcast_to(w[None], (NX,) + w.shape), "x", 0, 0)
    states, w4 = lax.optimization_barrier((states, w4))
    w_all = lax.all_gather(w4, ("z", "c")).reshape((NZ, NC) + w4.shape)
    part = width // N_CTX
    mine = lax.all_to_all(states.reshape(N_CTX, part, HEAD_DIM), ("x", "z"), 0, 0)
    scanned = pl.pallas_call(
        scan_kernel, out_shape=jax.ShapeDtypeStruct(mine.shape, BF), compiler_params=params(),
    )(mine)
    prefix = lax.all_to_all(scanned, ("x", "z"), 0, 0).reshape(width, HEAD_DIM)
    hidden = pl.pallas_call(
        attention_kernel,
        grid=(heads,),
        out_shape=jax.ShapeDtypeStruct((NY, rows, width), BF),
        in_specs=[by_head, by_head, by_head, state],
        out_specs=pl.BlockSpec((NY, rows, HEAD_DIM), lambda h: (0, 0, h)),
        compiler_params=params(),
    )(queries, keys, values, prefix)
    hidden = lax.all_to_all(hidden, "y", 0, 0)
    other = lax.ppermute(hidden, "c", [(0, 1), (1, 0)])
    return project(me_c.astype(jnp.int32).reshape(1), hidden, other, w_all)


def solution(mesh):
    fine = Mesh(mesh.devices.reshape(NX, NZ, NY, NC), AXES)
    ctx, head = ("x", "z"), ("y", "c")
    in_specs = (P(ctx, head), P(ctx, head), P(ctx, head), P(head, ctx))
    return jax.shard_map(local, mesh=fine, in_specs=in_specs, out_specs=P(ctx, head), check_vma=False)
```

```python
import jax
import jax.numpy as jnp
from jax import lax
from jax.experimental import pallas as pl
from jax.experimental.pallas import tpu as pltpu
from jax.sharding import Mesh, PartitionSpec as P

HEAD_DIM = 128
NX, NZ, NY, NC = 4, 16, 4, 2
N_CTX = NX * NZ
HOME = 2
BF = jnp.bfloat16
F32 = jnp.float32


def params():
    return pltpu.CompilerParams(vmem_limit_bytes=48 * 1024 * 1024)


def states_kernel(k_ref, v_ref, o_ref):
    o_ref[...] = lax.dot_general(
        k_ref[...], v_ref[...], (((0,), (0,)), ((), ())), preferred_element_type=F32
    ).astype(BF)


def scan_kernel(s_ref, o_ref):
    total = jnp.zeros(s_ref.shape[1:], F32)
    for c in range(s_ref.shape[0]):
        o_ref[c] = total.astype(BF)
        total = total + s_ref[c].astype(F32)


def intra_kernel(q_ref, k_ref, v_ref, o_ref):
    rows = q_ref.shape[0]
    blk = 256
    t = lax.broadcasted_iota(jnp.int32, (blk, blk), 0)
    s = lax.broadcasted_iota(jnp.int32, (blk, blk), 1)
    causal = t >= s
    for i in range(rows // blk):
        here = slice(i * blk, (i + 1) * blk)
        attn = None
        for j in range(i + 1):
            there = slice(j * blk, (j + 1) * blk)
            scores = lax.dot_general(
                q_ref[here, :], k_ref[there, :], (((1,), (1,)), ((), ())), preferred_element_type=F32
            )
            if i == j:
                scores = jnp.where(causal, scores, 0.0)
            part = jnp.dot(scores.astype(BF), v_ref[there, :], preferred_element_type=F32)
            attn = part if attn is None else attn + part
        o_ref[here, :] = attn


def attention_kernel(q_ref, i_ref, p_ref, o_ref):
    attn = i_ref[...] + jnp.dot(q_ref[...], p_ref[...], preferred_element_type=F32)
    scale = lax.rsqrt(jnp.mean(attn * attn, axis=-1, keepdims=True) + 1e-06)
    hidden = (attn * scale).astype(BF)
    for n in range(o_ref.shape[0]):
        o_ref[n] = hidden


def projection_kernel(core_ref, own_ref, far_ref, w_ref, o_ref, *scratch):
    parts, (other_ref, acc_ref, out_ref, sem) = scratch[:4], scratch[4:]
    core = core_ref[0]
    blocks, _, per, cols, depth = parts[0].shape
    rows_of = [(k, first) for k in range(NC) for first in range(0, NY, per)]
    copies = [
        pltpu.make_async_copy(
            w_ref.at[pl.ds(core * blocks, blocks), pl.ds(core ^ k, 1), pl.ds(first, per)], part, sem.at[n]
        )
        for n, ((k, first), part) in enumerate(zip(rows_of, parts))
    ]
    other = pltpu.make_async_copy(far_ref, other_ref, sem.at[len(copies)])
    halves = (pl.ds(0, o_ref.shape[0] // 2), pl.ds(o_ref.shape[0] // 2, o_ref.shape[0] // 2))
    outs = [pltpu.make_async_copy(out_ref.at[r], o_ref.at[r], sem.at[5 + n]) for n, r in enumerate(halves)]
    copies[0].start()
    copies[1].start()
    other.start()
    copies[2].start()
    copies[3].start()
    half = own_ref.shape[1] // 2
    for n, (k, first) in enumerate(rows_of):
        copies[n].wait()
        if n == len(rows_of) // NC:
            other.wait()
        h_ref = own_ref if k == 0 else other_ref
        last = n == len(rows_of) - 1
        for rows in (slice(0, half), slice(half, 2 * half)) if last else (slice(0, 2 * half),):
            total = None
            for i in range(per):
                w = parts[n][:, 0, i].reshape(blocks * cols, depth)
                h = h_ref[(first + i - HOME) % NY, rows]
                one = lax.dot_general(h, w, (((1,), (1,)), ((), ())), preferred_element_type=F32)
                total = one if total is None else total + one
            if n == 0:
                acc_ref[...] = total
            elif not last:
                acc_ref[...] += total
            else:
                out_ref[rows, :] = (acc_ref[rows, :] + total).astype(o_ref.dtype)
                outs[rows.start // half].start()
    for out in outs:
        out.wait()


def project(core, own, other, w_all):
    sources, rows, depth = own.shape
    cols = w_all.shape[3]
    blocks, per = NZ // NC, NY // 2
    anywhere, vmem = pl.BlockSpec(memory_space=pl.ANY), pl.BlockSpec(memory_space=pltpu.VMEM)
    return pl.pallas_call(
        projection_kernel,
        in_specs=[pl.BlockSpec(memory_space=pltpu.SMEM), vmem, anywhere, anywhere],
        out_specs=anywhere,
        scratch_shapes=[pltpu.VMEM((blocks, 1, per, cols, depth), BF)] * 4 + [
            pltpu.VMEM((sources, rows, depth), BF),
            pltpu.VMEM((rows, blocks * cols), F32),
            pltpu.VMEM((rows, blocks * cols), BF),
            pltpu.SemaphoreType.DMA((7,)),
        ],
        out_shape=jax.ShapeDtypeStruct((rows, blocks * cols), BF),
        compiler_params=params(),
    )(core, own, other, w_all)


AXES = ("x", "z", "y", "c")


def local(queries, keys, values, out_weight):
    rows, width = queries.shape
    heads = width // HEAD_DIM
    me_c = lax.axis_index("c")

    w = lax.ppermute(
        out_weight.T, ("x", "y"),
        [(x * NY + y, (y + HOME) % NX * NY + x) for x in range(NX) for y in range(NY)],
    )
    by_head = pl.BlockSpec((rows, HEAD_DIM), lambda h: (0, h))
    state = pl.BlockSpec((HEAD_DIM, HEAD_DIM), lambda h: (h, 0))
    states = pl.pallas_call(
        states_kernel,
        grid=(heads,),
        out_shape=jax.ShapeDtypeStruct((width, HEAD_DIM), BF),
        in_specs=[by_head, by_head], out_specs=state, compiler_params=params(),
    )(keys, values)
    states, w = lax.optimization_barrier((states, w))
    w4 = lax.all_to_all(jnp.broadcast_to(w[None], (NX,) + w.shape), "x", 0, 0)
    states, w4 = lax.optimization_barrier((states, w4))
    w_all = lax.all_gather(w4, ("z", "c")).reshape((NZ, NC) + w4.shape)
    intra = pl.pallas_call(
        intra_kernel,
        grid=(heads,),
        out_shape=jax.ShapeDtypeStruct((rows, width), F32),
        in_specs=[by_head] * 3, out_specs=by_head,
        cost_estimate=pl.CostEstimate(
            flops=4 * rows * rows * width, bytes_accessed=10 * rows * width, transcendentals=0
        ),
        compiler_params=params(),
    )(queries, keys, values)
    part = width // N_CTX
    mine = lax.all_to_all(states.reshape(N_CTX, part, HEAD_DIM), ("x", "z"), 0, 0)
    scanned = pl.pallas_call(
        scan_kernel, out_shape=jax.ShapeDtypeStruct(mine.shape, BF), compiler_params=params(),
    )(mine)
    prefix = lax.all_to_all(scanned, ("x", "z"), 0, 0).reshape(width, HEAD_DIM)
    hidden = pl.pallas_call(
        attention_kernel,
        grid=(heads,),
        out_shape=jax.ShapeDtypeStruct((NY, rows, width), BF),
        in_specs=[by_head, by_head, state],
        out_specs=pl.BlockSpec((NY, rows, HEAD_DIM), lambda h: (0, 0, h)),
        compiler_params=params(),
    )(queries, intra, prefix)
    hidden = lax.all_to_all(hidden, "y", 0, 0)
    other = lax.ppermute(hidden, "c", [(0, 1), (1, 0)])
    return project(me_c.astype(jnp.int32).reshape(1), hidden, other, w_all)


def solution(mesh):
    fine = Mesh(mesh.devices.reshape(NX, NZ, NY, NC), AXES)
    ctx, head = ("x", "z"), ("y", "c")
    in_specs = (P(ctx, head), P(ctx, head), P(ctx, head), P(head, ctx))
    return jax.shard_map(local, mesh=fine, in_specs=in_specs, out_specs=P(ctx, head), check_vma=False)
```

```python
import jax
import jax.numpy as jnp
from jax import lax
from jax.experimental import pallas as pl
from jax.experimental.pallas import tpu as pltpu
from jax.sharding import Mesh, PartitionSpec as P

HEAD_DIM = 128
NX, NZ, NY, NC = 4, 16, 4, 2
N_CTX = NX * NZ
HOME = 2
BF = jnp.bfloat16
F32 = jnp.float32


def params():
    return pltpu.CompilerParams(vmem_limit_bytes=48 * 1024 * 1024)


def states_kernel(k_ref, v_ref, o_ref):
    o_ref[...] = lax.dot_general(
        k_ref[...], v_ref[...], (((0,), (0,)), ((), ())), preferred_element_type=F32
    ).astype(BF)


def scan_kernel(s_ref, o_ref):
    total = jnp.zeros(s_ref.shape[1:], F32)
    for c in range(s_ref.shape[0]):
        o_ref[c] = total.astype(BF)
        total = total + s_ref[c].astype(F32)


def intra_kernel(q_ref, k_ref, v_ref, o_ref):
    rows = q_ref.shape[0]
    blk = 256
    t = lax.broadcasted_iota(jnp.int32, (blk, blk), 0)
    s = lax.broadcasted_iota(jnp.int32, (blk, blk), 1)
    causal = t >= s
    for i in range(rows // blk):
        here = slice(i * blk, (i + 1) * blk)
        attn = None
        for j in range(i + 1):
            there = slice(j * blk, (j + 1) * blk)
            scores = lax.dot_general(
                q_ref[here, :], k_ref[there, :], (((1,), (1,)), ((), ())), preferred_element_type=F32
            )
            if i == j:
                scores = jnp.where(causal, scores, 0.0)
            part = jnp.dot(scores.astype(BF), v_ref[there, :], preferred_element_type=F32)
            attn = part if attn is None else attn + part
        o_ref[here, :] = attn


def attention_kernel(q_ref, i_ref, p_ref, o_ref):
    attn = i_ref[...] + jnp.dot(q_ref[...], p_ref[...], preferred_element_type=F32)
    scale = lax.rsqrt(jnp.mean(attn * attn, axis=-1, keepdims=True) + 1e-06)
    hidden = (attn * scale).astype(BF)
    for n in range(o_ref.shape[0]):
        o_ref[n] = hidden


def projection_kernel(core_ref, own_ref, far_ref, w_ref, o_ref, *scratch):
    parts, other_ref, acc_ref, sem = scratch[:4], scratch[4], scratch[5], scratch[6]
    core = core_ref[0]
    blocks, _, per, cols, depth = parts[0].shape
    rows_of = [(k, first) for k in range(NC) for first in range(0, NY, per)]
    copies = [
        pltpu.make_async_copy(
            w_ref.at[pl.ds(core * blocks, blocks), pl.ds(core ^ k, 1), pl.ds(first, per)], part, sem.at[n]
        )
        for n, ((k, first), part) in enumerate(zip(rows_of, parts))
    ]
    other = pltpu.make_async_copy(far_ref, other_ref, sem.at[len(copies)])
    copies[0].start()
    copies[1].start()
    other.start()
    copies[2].start()
    copies[3].start()
    for n, (k, first) in enumerate(rows_of):
        copies[n].wait()
        if n == len(rows_of) // NC:
            other.wait()
        h_ref = own_ref if k == 0 else other_ref
        total = None
        for i in range(per):
            w = parts[n][:, 0, i].reshape(blocks * cols, depth)
            one = lax.dot_general(
                h_ref[(first + i - HOME) % NY], w, (((1,), (1,)), ((), ())), preferred_element_type=F32
            )
            total = one if total is None else total + one
        if n == 0:
            acc_ref[...] = total
        elif n < len(rows_of) - 1:
            acc_ref[...] += total
        else:
            o_ref[...] = (acc_ref[...] + total).astype(o_ref.dtype)


def project(core, own, other, w_all):
    sources, rows, depth = own.shape
    cols = w_all.shape[3]
    blocks, per = NZ // NC, NY // 2
    anywhere, vmem = pl.BlockSpec(memory_space=pl.ANY), pl.BlockSpec(memory_space=pltpu.VMEM)
    return pl.pallas_call(
        projection_kernel,
        in_specs=[pl.BlockSpec(memory_space=pltpu.SMEM), vmem, anywhere, anywhere],
        out_specs=vmem,
        scratch_shapes=[pltpu.VMEM((blocks, 1, per, cols, depth), BF)] * 4 + [
            pltpu.VMEM((sources, rows, depth), BF),
            pltpu.VMEM((rows, blocks * cols), F32),
            pltpu.SemaphoreType.DMA((5,)),
        ],
        out_shape=jax.ShapeDtypeStruct((rows, blocks * cols), BF),
        compiler_params=params(),
    )(core, own, other, w_all)


AXES = ("x", "z", "y", "c")


def local(queries, keys, values, out_weight):
    rows, width = queries.shape
    heads = width // HEAD_DIM
    me_c = lax.axis_index("c")

    w = lax.ppermute(
        out_weight.T, ("x", "y"),
        [(x * NY + y, (y + HOME) % NX * NY + x) for x in range(NX) for y in range(NY)],
    )
    by_head = pl.BlockSpec((rows, HEAD_DIM), lambda h: (0, h))
    state = pl.BlockSpec((HEAD_DIM, HEAD_DIM), lambda h: (h, 0))
    states = pl.pallas_call(
        states_kernel,
        grid=(heads,),
        out_shape=jax.ShapeDtypeStruct((width, HEAD_DIM), BF),
        in_specs=[by_head, by_head], out_specs=state, compiler_params=params(),
    )(keys, values)
    states, w = lax.optimization_barrier((states, w))
    w4 = lax.all_to_all(jnp.broadcast_to(w[None], (NX,) + w.shape), "x", 0, 0)
    states, w4 = lax.optimization_barrier((states, w4))
    w_all = lax.all_gather(w4, ("z", "c")).reshape((NZ, NC) + w4.shape)
    intra = pl.pallas_call(
        intra_kernel,
        grid=(heads,),
        out_shape=jax.ShapeDtypeStruct((rows, width), F32),
        in_specs=[by_head] * 3, out_specs=by_head,
        cost_estimate=pl.CostEstimate(
            flops=4 * rows * rows * width, bytes_accessed=10 * rows * width, transcendentals=0
        ),
        compiler_params=params(),
    )(queries, keys, values)
    part = width // N_CTX
    mine = lax.all_to_all(states.reshape(N_CTX, part, HEAD_DIM), ("x", "z"), 0, 0)
    scanned = pl.pallas_call(
        scan_kernel, out_shape=jax.ShapeDtypeStruct(mine.shape, BF), compiler_params=params(),
    )(mine)
    prefix = lax.all_to_all(scanned, ("x", "z"), 0, 0).reshape(width, HEAD_DIM)
    hidden = pl.pallas_call(
        attention_kernel,
        grid=(heads,),
        out_shape=jax.ShapeDtypeStruct((NY, rows, width), BF),
        in_specs=[by_head, by_head, state],
        out_specs=pl.BlockSpec((NY, rows, HEAD_DIM), lambda h: (0, 0, h)),
        compiler_params=params(),
    )(queries, intra, prefix)
    hidden = lax.all_to_all(hidden, "y", 0, 0)
    other = lax.ppermute(hidden, "c", [(0, 1), (1, 0)])
    return project(me_c.astype(jnp.int32).reshape(1), hidden, other, w_all)


def solution(mesh):
    fine = Mesh(mesh.devices.reshape(NX, NZ, NY, NC), AXES)
    ctx, head = ("x", "z"), ("y", "c")
    in_specs = (P(ctx, head), P(ctx, head), P(ctx, head), P(head, ctx))
    return jax.shard_map(local, mesh=fine, in_specs=in_specs, out_specs=P(ctx, head), check_vma=False)
```

```python
import jax
import jax.numpy as jnp
from jax import lax
from jax.experimental import pallas as pl
from jax.experimental.pallas import tpu as pltpu
from jax.sharding import Mesh, PartitionSpec as P

HEAD_DIM = 128
NX, NZ, NY, NC = 4, 16, 4, 2
N_CTX = NX * NZ
HOME = 2
BF = jnp.bfloat16
F32 = jnp.float32


def params():
    return pltpu.CompilerParams(vmem_limit_bytes=48 * 1024 * 1024)


def states_kernel(k_ref, v_ref, o_ref):
    o_ref[...] = lax.dot_general(
        k_ref[...], v_ref[...], (((0,), (0,)), ((), ())), preferred_element_type=F32
    ).astype(BF)


def scan_kernel(s_ref, o_ref):
    total = jnp.zeros(s_ref.shape[1:], F32)
    for c in range(s_ref.shape[0]):
        o_ref[c] = total.astype(BF)
        total = total + s_ref[c].astype(F32)


def attention_kernel(q_ref, k_ref, v_ref, p_ref, o_ref):
    rows = q_ref.shape[0]
    blk = 256
    t = lax.broadcasted_iota(jnp.int32, (blk, blk), 0)
    s = lax.broadcasted_iota(jnp.int32, (blk, blk), 1)
    causal = t >= s
    prefix = p_ref[...]
    for i in range(rows // blk):
        here = slice(i * blk, (i + 1) * blk)
        q = q_ref[here, :]
        attn = jnp.dot(q, prefix, preferred_element_type=F32)
        for j in range(i + 1):
            there = slice(j * blk, (j + 1) * blk)
            scores = lax.dot_general(
                q, k_ref[there, :], (((1,), (1,)), ((), ())), preferred_element_type=F32
            )
            if i == j:
                scores = jnp.where(causal, scores, 0.0)
            attn += jnp.dot(scores.astype(BF), v_ref[there, :], preferred_element_type=F32)
        scale = lax.rsqrt(jnp.mean(attn * attn, axis=-1, keepdims=True) + 1e-06)
        hidden = (attn * scale).astype(BF)
        for n in range(o_ref.shape[0]):
            o_ref[n, here, :] = hidden


def projection_kernel(core_ref, own_ref, far_ref, w_ref, o_ref, *scratch):
    parts, (other_ref, acc_ref, out_ref, sem) = scratch[:4], scratch[4:]
    core = core_ref[0]
    blocks, _, per, cols, depth = parts[0].shape
    rows_of = [(k, first) for k in range(NC) for first in range(0, NY, per)]
    copies = [
        pltpu.make_async_copy(
            w_ref.at[pl.ds(core * blocks, blocks), pl.ds(core ^ k, 1), pl.ds(first, per)], part, sem.at[n]
        )
        for n, ((k, first), part) in enumerate(zip(rows_of, parts))
    ]
    other = pltpu.make_async_copy(far_ref, other_ref, sem.at[len(copies)])
    halves = (pl.ds(0, o_ref.shape[0] // 2), pl.ds(o_ref.shape[0] // 2, o_ref.shape[0] // 2))
    outs = [pltpu.make_async_copy(out_ref.at[r], o_ref.at[r], sem.at[5 + n]) for n, r in enumerate(halves)]
    copies[0].start()
    copies[1].start()
    other.start()
    copies[2].start()
    copies[3].start()
    half = own_ref.shape[1] // 2
    for n, (k, first) in enumerate(rows_of):
        copies[n].wait()
        if n == len(rows_of) // NC:
            other.wait()
        h_ref = own_ref if k == 0 else other_ref
        last = n == len(rows_of) - 1
        for rows in (slice(0, half), slice(half, 2 * half)) if last else (slice(0, 2 * half),):
            total = None
            for i in range(per):
                w = parts[n][:, 0, i].reshape(blocks * cols, depth)
                h = h_ref[(first + i - HOME) % NY, rows]
                one = lax.dot_general(h, w, (((1,), (1,)), ((), ())), preferred_element_type=F32)
                total = one if total is None else total + one
            if n == 0:
                acc_ref[...] = total
            elif not last:
                acc_ref[...] += total
            else:
                out_ref[rows, :] = (acc_ref[rows, :] + total).astype(o_ref.dtype)
                outs[rows.start // half].start()
    for out in outs:
        out.wait()


def project(core, own, other, w_all):
    sources, rows, depth = own.shape
    cols = w_all.shape[3]
    blocks, per = NZ // NC, NY // 2
    anywhere, vmem = pl.BlockSpec(memory_space=pl.ANY), pl.BlockSpec(memory_space=pltpu.VMEM)
    return pl.pallas_call(
        projection_kernel,
        in_specs=[pl.BlockSpec(memory_space=pltpu.SMEM), vmem, anywhere, anywhere],
        out_specs=anywhere,
        scratch_shapes=[pltpu.VMEM((blocks, 1, per, cols, depth), BF)] * 4 + [
            pltpu.VMEM((sources, rows, depth), BF),
            pltpu.VMEM((rows, blocks * cols), F32),
            pltpu.VMEM((rows, blocks * cols), BF),
            pltpu.SemaphoreType.DMA((7,)),
        ],
        out_shape=jax.ShapeDtypeStruct((rows, blocks * cols), BF),
        compiler_params=params(),
    )(core, own, other, w_all)


AXES = ("x", "z", "y", "c")


def local(queries, keys, values, out_weight):
    rows, width = queries.shape
    heads = width // HEAD_DIM
    me_c = lax.axis_index("c")

    w = lax.ppermute(
        out_weight.T, ("x", "y"),
        [(x * NY + y, (y + HOME) % NX * NY + x) for x in range(NX) for y in range(NY)],
    )
    by_head = pl.BlockSpec((rows, HEAD_DIM), lambda h: (0, h))
    state = pl.BlockSpec((HEAD_DIM, HEAD_DIM), lambda h: (h, 0))
    states = pl.pallas_call(
        states_kernel,
        grid=(heads,),
        out_shape=jax.ShapeDtypeStruct((width, HEAD_DIM), BF),
        in_specs=[by_head, by_head], out_specs=state, compiler_params=params(),
    )(keys, values)
    states, w = lax.optimization_barrier((states, w))
    w4 = lax.all_to_all(jnp.broadcast_to(w[None], (NX,) + w.shape), "x", 0, 0)
    states, w4 = lax.optimization_barrier((states, w4))
    w_all = lax.all_gather(w4, ("z", "c")).reshape((NZ, NC) + w4.shape)
    part = width // N_CTX
    mine = lax.all_to_all(states.reshape(N_CTX, part, HEAD_DIM), ("x", "z"), 0, 0)
    scanned = pl.pallas_call(
        scan_kernel, out_shape=jax.ShapeDtypeStruct(mine.shape, BF), compiler_params=params(),
    )(mine)
    prefix = lax.all_to_all(scanned, ("x", "z"), 0, 0).reshape(width, HEAD_DIM)
    hidden = pl.pallas_call(
        attention_kernel,
        grid=(heads,),
        out_shape=jax.ShapeDtypeStruct((NY, rows, width), BF),
        in_specs=[by_head, by_head, by_head, state],
        out_specs=pl.BlockSpec((NY, rows, HEAD_DIM), lambda h: (0, 0, h)),
        compiler_params=params(),
    )(queries, keys, values, prefix)
    hidden = lax.all_to_all(hidden, "y", 0, 0)
    other = lax.ppermute(hidden, "c", [(0, 1), (1, 0)])
    return project(me_c.astype(jnp.int32).reshape(1), hidden, other, w_all)


def solution(mesh):
    fine = Mesh(mesh.devices.reshape(NX, NZ, NY, NC), AXES)
    ctx, head = ("x", "z"), ("y", "c")
    in_specs = (P(ctx, head), P(ctx, head), P(ctx, head), P(head, ctx))
    return jax.shard_map(local, mesh=fine, in_specs=in_specs, out_specs=P(ctx, head), check_vma=False)
```

```python
import jax
import jax.numpy as jnp
from jax import lax
from jax.experimental import pallas as pl
from jax.experimental.pallas import tpu as pltpu
from jax.sharding import Mesh, PartitionSpec as P

HEAD_DIM = 128
NX, NZ, NY, NC = 4, 16, 4, 2
N_CTX = NX * NZ
HOME = 2
PARTS = ((0, 0, 1), (0, 1, 3), (1, 0, 2), (1, 2, 2))
BF = jnp.bfloat16
F32 = jnp.float32


def params():
    return pltpu.CompilerParams(vmem_limit_bytes=48 * 1024 * 1024)


def states_kernel(k_ref, v_ref, o_ref):
    o_ref[...] = lax.dot_general(
        k_ref[...], v_ref[...], (((0,), (0,)), ((), ())), preferred_element_type=F32
    ).astype(BF)


def scan_kernel(s_ref, o_ref):
    total = jnp.zeros(s_ref.shape[1:], F32)
    for c in range(s_ref.shape[0]):
        o_ref[c] = total.astype(BF)
        total = total + s_ref[c].astype(F32)


def attention_kernel(q_ref, k_ref, v_ref, p_ref, o_ref):
    rows = q_ref.shape[0]
    blk = 256
    t = lax.broadcasted_iota(jnp.int32, (blk, blk), 0)
    s = lax.broadcasted_iota(jnp.int32, (blk, blk), 1)
    causal = t >= s
    prefix = p_ref[...]
    for i in range(rows // blk):
        here = slice(i * blk, (i + 1) * blk)
        q = q_ref[here, :]
        attn = jnp.dot(q, prefix, preferred_element_type=F32)
        for j in range(i + 1):
            there = slice(j * blk, (j + 1) * blk)
            scores = lax.dot_general(
                q, k_ref[there, :], (((1,), (1,)), ((), ())), preferred_element_type=F32
            )
            if i == j:
                scores = jnp.where(causal, scores, 0.0)
            attn += jnp.dot(scores.astype(BF), v_ref[there, :], preferred_element_type=F32)
        scale = lax.rsqrt(jnp.mean(attn * attn, axis=-1, keepdims=True) + 1e-06)
        hidden = (attn * scale).astype(BF)
        for n in range(o_ref.shape[0]):
            o_ref[n, here, :] = hidden


def projection_kernel(core_ref, own_ref, far_ref, w_ref, o_ref, *scratch):
    parts, (other_ref, acc_ref, out_ref, sem) = scratch[:len(PARTS)], scratch[len(PARTS):]
    core = core_ref[0]
    blocks, _, _, cols, depth = parts[0].shape
    copies = [
        pltpu.make_async_copy(
            w_ref.at[pl.ds(core * blocks, blocks), pl.ds(core ^ k, 1), pl.ds(first, per)], part, sem.at[n]
        )
        for n, ((k, first, per), part) in enumerate(zip(PARTS, parts))
    ]
    other = pltpu.make_async_copy(far_ref, other_ref, sem.at[len(copies)])
    halves = (pl.ds(0, o_ref.shape[0] // 2), pl.ds(o_ref.shape[0] // 2, o_ref.shape[0] // 2))
    outs = [pltpu.make_async_copy(out_ref.at[r], o_ref.at[r], sem.at[len(copies) + 1 + n]) for n, r in enumerate(halves)]
    for copy in copies[:2] + [other] + copies[2:]:
        copy.start()
    half = own_ref.shape[1] // 2
    for n, (k, first, per) in enumerate(PARTS):
        copies[n].wait()
        if n == 2:
            other.wait()
        h_ref = own_ref if k == 0 else other_ref
        last = n == len(PARTS) - 1
        for rows in (slice(0, half), slice(half, 2 * half)) if last else (slice(0, 2 * half),):
            total = None
            for i in range(per):
                w = parts[n][:, 0, i].reshape(blocks * cols, depth)
                h = h_ref[(first + i - HOME) % NY, rows]
                one = lax.dot_general(h, w, (((1,), (1,)), ((), ())), preferred_element_type=F32)
                total = one if total is None else total + one
            if n == 0:
                acc_ref[...] = total
            elif not last:
                acc_ref[...] += total
            else:
                out_ref[rows, :] = (acc_ref[rows, :] + total).astype(o_ref.dtype)
                outs[rows.start // half].start()
    for out in outs:
        out.wait()


def project(core, own, other, w_all):
    sources, rows, depth = own.shape
    cols = w_all.shape[3]
    blocks = NZ // NC
    anywhere, vmem = pl.BlockSpec(memory_space=pl.ANY), pl.BlockSpec(memory_space=pltpu.VMEM)
    return pl.pallas_call(
        projection_kernel,
        in_specs=[pl.BlockSpec(memory_space=pltpu.SMEM), vmem, anywhere, anywhere],
        out_specs=anywhere,
        scratch_shapes=[pltpu.VMEM((blocks, 1, per, cols, depth), BF) for _, _, per in PARTS] + [
            pltpu.VMEM((sources, rows, depth), BF),
            pltpu.VMEM((rows, blocks * cols), F32),
            pltpu.VMEM((rows, blocks * cols), BF),
            pltpu.SemaphoreType.DMA((7,)),
        ],
        out_shape=jax.ShapeDtypeStruct((rows, blocks * cols), BF),
        compiler_params=params(),
    )(core, own, other, w_all)


AXES = ("x", "z", "y", "c")


def local(queries, keys, values, out_weight):
    rows, width = queries.shape
    heads = width // HEAD_DIM
    me_c = lax.axis_index("c")

    w = lax.ppermute(
        out_weight.T, ("x", "y"),
        [(x * NY + y, (y + HOME) % NX * NY + x) for x in range(NX) for y in range(NY)],
    )
    by_head = pl.BlockSpec((rows, HEAD_DIM), lambda h: (0, h))
    state = pl.BlockSpec((HEAD_DIM, HEAD_DIM), lambda h: (h, 0))
    states = pl.pallas_call(
        states_kernel,
        grid=(heads,),
        out_shape=jax.ShapeDtypeStruct((width, HEAD_DIM), BF),
        in_specs=[by_head, by_head], out_specs=state, compiler_params=params(),
    )(keys, values)
    states, w = lax.optimization_barrier((states, w))
    w4 = lax.all_to_all(jnp.broadcast_to(w[None], (NX,) + w.shape), "x", 0, 0)
    states, w4 = lax.optimization_barrier((states, w4))
    w_all = lax.all_gather(w4, ("z", "c")).reshape((NZ, NC) + w4.shape)
    part = width // N_CTX
    mine = lax.all_to_all(states.reshape(N_CTX, part, HEAD_DIM), ("x", "z"), 0, 0)
    scanned = pl.pallas_call(
        scan_kernel, out_shape=jax.ShapeDtypeStruct(mine.shape, BF), compiler_params=params(),
    )(mine)
    prefix = lax.all_to_all(scanned, ("x", "z"), 0, 0).reshape(width, HEAD_DIM)
    hidden = pl.pallas_call(
        attention_kernel,
        grid=(heads,),
        out_shape=jax.ShapeDtypeStruct((NY, rows, width), BF),
        in_specs=[by_head, by_head, by_head, state],
        out_specs=pl.BlockSpec((NY, rows, HEAD_DIM), lambda h: (0, 0, h)),
        compiler_params=params(),
    )(queries, keys, values, prefix)
    hidden = lax.all_to_all(hidden, "y", 0, 0)
    other = lax.ppermute(hidden, "c", [(0, 1), (1, 0)])
    return project(me_c.astype(jnp.int32).reshape(1), hidden, other, w_all)


def solution(mesh):
    fine = Mesh(mesh.devices.reshape(NX, NZ, NY, NC), AXES)
    ctx, head = ("x", "z"), ("y", "c")
    in_specs = (P(ctx, head), P(ctx, head), P(ctx, head), P(head, ctx))
    return jax.shard_map(local, mesh=fine, in_specs=in_specs, out_specs=P(ctx, head), check_vma=False)
```
